32 devices in a mesh: parts: 2 (over y), blk: 2 (over core), group: 8 (over z, x).
Axes of the slice: x: 2, y: 2, z: 4, core: 2. Of those that a mesh axis runs over, the one named last changes fastest.
Arguments:
- img_student: bfloat16 [2048, 256], P(('parts', 'group')), parts along dimension 0, may hold values from -25 to 25
- txt_student: bfloat16 [2048, 256], P(('parts', 'group')), parts along dimension 0, may hold values from -25 to 25
- img_teacher: bfloat16 [2048, 512], P(('parts', 'group')), parts along dimension 0, may hold values from -25 to 25
- txt_teacher: bfloat16 [2048, 512], P(('parts', 'group')), parts along dimension 0, may hold values from -25 to 25
Outputs:
- grad_image: float32 [2048, 256], P(('parts', 'group')), parts along dimension 0
The draws below stay inside these ranges and needn't reach their ends.
There are 2 independent parts, one for each index of `parts`. The reference program is written for one: setup_inputs(seed, part) draws one part's arguments, and reference() takes and returns one part's arrays. A program takes and returns all parts, laid end to end along the dimension named above; each array names one. Nothing has to cross between parts.
All inputs are finite; a program needn't handle non-finite values.
Results may differ from the reference program's by a relative error of at most 0.0028.
Values may be sent and summed in bfloat16 or wider, within the bound.
A program may use at most 128 MiB of HBM per device.

```python
import jax
import jax.numpy as jnp

STUDENT_DIM = 256
TEACHER_DIM = 512
BATCH = 1024


def draw_img_student(key, part):
    key = jax.random.fold_in(key, 1)
    return jnp.clip(jax.random.normal(key, (BATCH, STUDENT_DIM)) * 0.45, -2.7, 2.7).astype(jnp.bfloat16)


def draw_txt_student(key, part):
    key = jax.random.fold_in(key, 2)
    return jnp.clip(jax.random.normal(key, (BATCH, STUDENT_DIM)) * 0.45, -2.7, 2.7).astype(jnp.bfloat16)


def draw_img_teacher(key, part):
    key = jax.random.fold_in(key, 3)
    return jnp.clip(jax.random.normal(key, (BATCH, TEACHER_DIM)) * 0.37, -2.22, 2.22).astype(jnp.bfloat16)


def draw_txt_teacher(key, part):
    key = jax.random.fold_in(key, 4)
    return jnp.clip(jax.random.normal(key, (BATCH, TEACHER_DIM)) * 0.37, -2.22, 2.22).astype(jnp.bfloat16)


def setup_inputs(seed: int = 0, part: int = 0) -> dict:
    keys = jax.random.split(jax.random.key(seed), 5)
    own_keys = jax.random.split(jax.random.fold_in(keys[4], part), 5)
    return {
        "img_student": draw_img_student(jax.random.fold_in(jax.random.fold_in(keys[4], part), 71), part),
        "txt_student": draw_txt_student(jax.random.fold_in(jax.random.fold_in(keys[4], part), 71), part),
        "img_teacher": draw_img_teacher(jax.random.fold_in(jax.random.fold_in(keys[4], part), 71), part),
        "txt_teacher": draw_txt_teacher(jax.random.fold_in(jax.random.fold_in(keys[4], part), 71), part),
    }


def log_total(logits, axis):
    highest = jnp.max(logits, axis=axis, keepdims=True)
    return highest + jnp.log(jnp.sum(jnp.exp(logits - highest), axis=axis, keepdims=True))


def reference(img_student, txt_student, img_teacher, txt_teacher):
    student = jnp.dot(img_student, txt_student.T, preferred_element_type=jnp.float32)
    teacher = jnp.dot(img_teacher, txt_teacher.T, preferred_element_type=jnp.float32)
    row_part = jnp.exp(student - log_total(student, 1)) - jnp.exp(teacher - log_total(teacher, 1))
    column_part = jnp.exp(student - log_total(student, 0)) - jnp.exp(teacher - log_total(teacher, 0))
    weights = (0.5 * (row_part + column_part)).astype(jnp.bfloat16)
    return jnp.dot(weights, txt_student, preferred_element_type=jnp.float32)
```

```python
import functools

import jax
import jax.numpy as jnp
from jax import lax
from jax.experimental import pallas as pl
from jax.experimental.pallas import tpu as pltpu
from jax.sharding import PartitionSpec as P


def merged_2(value, axis, join):
    pieces = jax.tree.map(lambda part: lax.all_gather(part, axis), value)
    head = jax.tree.map(lambda part: part[0], pieces)
    tail = jax.tree.map(lambda part: part[1:], pieces)
    so_far, _ = lax.scan(lambda so_far, piece: (join(so_far, piece), None), head, tail)
    return so_far


def combine(earlier, later):
    merged = []
    for which in (0, 2):
        highest = jnp.maximum(earlier[which], later[which])
        total = earlier[which + 1] * jnp.exp(earlier[which] - highest) + later[which + 1] * jnp.exp(
            later[which] - highest
        )
        merged.append(highest)
        merged.append(total)
    return tuple(merged)


def general(img_student, txt_student, img_teacher, txt_teacher):
    half_rows = img_student.shape[0] // 2
    side = lax.axis_index("blk")
    begin = side * half_rows
    text_student_own = lax.dynamic_slice_in_dim(txt_student, begin, half_rows, 0)
    text_teacher_own = lax.dynamic_slice_in_dim(txt_teacher, begin, half_rows, 0)
    contract = (((1,), (1,)), ((), ()))
    text_student, text_teacher = (
        lax.all_gather(text_student_own, "group", axis=0, tiled=True),
        lax.all_gather(text_teacher_own, "group", axis=0, tiled=True),
    )
    student = lax.dot_general(
        img_student, text_student, contract, preferred_element_type=jnp.float32
    )
    teacher = lax.dot_general(
        img_teacher, text_teacher, contract, preferred_element_type=jnp.float32
    )
    row_student_high = jnp.max(student, axis=1)
    row_teacher_high = jnp.max(teacher, axis=1)
    row_stats = (
        row_student_high,
        jnp.sum(jnp.exp(student - row_student_high[:, None]), axis=1),
        row_teacher_high,
        jnp.sum(jnp.exp(teacher - row_teacher_high[:, None]), axis=1),
    )
    row_all = merged_2(row_stats, "blk", combine)
    row_student = (row_all[0] + jnp.log(row_all[1]))[:, None]
    row_teacher = (row_all[2] + jnp.log(row_all[3]))[:, None]
    column_student_high = jnp.max(student, axis=0)
    column_teacher_high = jnp.max(teacher, axis=0)
    column_stats = (
        column_student_high,
        jnp.sum(jnp.exp(student - column_student_high[None, :]), axis=0),
        column_teacher_high,
        jnp.sum(jnp.exp(teacher - column_teacher_high[None, :]), axis=0),
    )
    totals = merged_2(column_stats, "group", combine)
    column_student = (totals[0] + jnp.log(totals[1]))[None, :]
    column_teacher = (totals[2] + jnp.log(totals[3]))[None, :]
    row_part = jnp.exp(student - row_student) - jnp.exp(teacher - row_teacher)
    column_part = jnp.exp(student - column_student) - jnp.exp(teacher - column_teacher)
    weights = (0.5 * (row_part + column_part)).astype(jnp.bfloat16)
    partial_image = jnp.dot(weights, text_student, preferred_element_type=jnp.float32)
    return lax.psum(partial_image, "blk")


MESH = pl.DeviceIdType.MESH
SQUARE = 4


def exchange_kernel(
    img_s_hbm, txt_s_hbm, img_t_hbm, txt_t_hbm, out_ref,
    txt_s, txt_t, img_s, img_t,
    er_s, er_t, ec_s, ec_t,
    col_stats, row_send, row_recv, part_a, part_b, part_c,
    local_sem,
    txt_send, txt_recv, fwd_send, fwd_recv,
    img_send, img_recv,
    col_send, col_recv, row_send_sem, row_recv_sem,
    a_send, a_recv, b_send, b_recv,
):
    rows = img_s.shape[0]
    half = rows // 2
    group = lax.axis_index("group")
    core = lax.axis_index("blk")
    x = lax.rem(group, 2)
    b = lax.rem(group // 2, 2)
    a = group // 4

    def chip(d, other_half=0):
        return (
            lax.rem(a + other_half, 2) * 4
            + lax.rem(b + d // 2, 2) * 2
            + lax.rem(x + d % 2, 2)
        )

    def device(chip_index, core_index):
        return {"blk": core_index, "group": chip_index}

    sibling = device(group, 1 - core)
    partner = chip(0, 1)

    def remote(src, dst, send, recv, target):
        return pltpu.make_async_remote_copy(
            src_ref=src, dst_ref=dst, send_sem=send, recv_sem=recv,
            device_id=target, device_id_type=MESH,
        )

    mine = pl.ds(pl.multiple_of(core * half, half), half)
    theirs = pl.ds(pl.multiple_of((1 - core) * half, half), half)

    own = [
        pltpu.make_async_copy(txt_s_hbm, txt_s.at[0], local_sem.at[0]),
        pltpu.make_async_copy(txt_t_hbm, txt_t.at[0], local_sem.at[1]),
    ]
    own_img = [
        pltpu.make_async_copy(img_s_hbm, img_s, local_sem.at[2]),
        pltpu.make_async_copy(img_t_hbm, img_t, local_sem.at[3]),
    ]
    for copy in own:
        copy.start()

    @pl.when(core == 0)
    def _():
        for copy in own_img:
            copy.start()

    barrier = pltpu.get_barrier_semaphore()
    greeted = [sibling, device(partner, core), device(partner, 1 - core)]
    for d in range(1, SQUARE):
        greeted += [device(chip(d), core), device(chip(d), 1 - core)]
    for target in greeted:
        pl.semaphore_signal(barrier, inc=1, device_id=target, device_id_type=MESH)
    pl.semaphore_wait(barrier, len(greeted))

    img_out = [
        remote(img_s_hbm.at[mine], img_s.at[mine], img_send.at[0], img_recv.at[0, core], device(partner, 1)),
        remote(img_t_hbm.at[mine], img_t.at[mine], img_send.at[1], img_recv.at[1, core], device(partner, 1)),
    ]
    text_out = {}
    for d in range(1, SQUARE):
        text_out[d] = [
            remote(txt_s_hbm.at[mine], txt_s.at[d, mine], txt_send.at[0, d], txt_recv.at[0, d], device(chip(d), core)),
            remote(txt_t_hbm.at[mine], txt_t.at[d, mine], txt_send.at[1, d], txt_recv.at[1, d], device(chip(d), core)),
        ]
    img_out[0].start()
    for copy in text_out[1] + text_out[2]:
        copy.start()
    img_out[1].start()
    for copy in text_out[3]:
        copy.start()

    forward = {}

    def pass_on(d):
        forward[d] = []
        for which, ref in ((0, txt_s), (1, txt_t)):
            text_out[d][which].wait_recv()
            copy = remote(
                ref.at[d, mine], ref.at[d, mine],
                fwd_send.at[which, d], fwd_recv.at[which, d], sibling,
            )
            copy.start()
            forward[d].append(copy)

    contract = (((1,), (1,)), ((), ()))
    row_stats = []

    def tile(d):
        if d == 0:
            for copy in own:
                copy.wait()
        else:
            for which, ref in ((0, txt_s), (1, txt_t)):
                remote(
                    ref.at[d, theirs], ref.at[d, theirs],
                    fwd_send.at[which, d], fwd_recv.at[which, d], sibling,
                ).wait_recv()
        found = []
        for which, (img, txt, er, ec) in enumerate(
            ((img_s, txt_s, er_s, ec_s), (img_t, txt_t, er_t, ec_t))
        ):
            logits = lax.dot_general(
                img[...], txt[d], contract, preferred_element_type=jnp.float32
            )
            row_high = jnp.max(logits, axis=1, keepdims=True)
            row_exp = jnp.exp(logits - row_high)
            er[d] = row_exp
            found.append((row_high, jnp.sum(row_exp, axis=1, keepdims=True)))
            column_high = jnp.max(logits, axis=0, keepdims=True)
            column_exp = jnp.exp(logits - column_high)
            ec[d] = column_exp
            at = which * SQUARE + d
            col_stats[0, at : at + 1, :] = column_high
            col_stats[0, 8 + at : 9 + at, :] = jnp.sum(column_exp, axis=0, keepdims=True)
        row_stats.append(found)

    pass_on(1)

    @pl.when(core == 0)
    def _():
        for copy in own_img:
            copy.wait()

    @pl.when(core == 1)
    def _():
        for h in range(2):
            at = pl.ds(h * half, half)
            for which, ref in ((0, img_s), (1, img_t)):
                remote(
                    ref.at[at], ref.at[at], img_send.at[which], img_recv.at[which, h], device(partner, 1)
                ).wait_recv()

    tile(0)
    pass_on(2)
    tile(1)
    pass_on(3)
    tile(2)
    tile(3)

    col_out = []
    for d in range(SQUARE):
        for e in range(2):
            slot = 2 * d + e
            if slot:
                target = device(chip(d), core if e == 0 else 1 - core)
                copy = remote(
                    col_stats.at[0], col_stats.at[slot], col_send.at[slot], col_recv.at[slot], target
                )
                copy.start()
                col_out.append(copy)

    lane = lax.broadcasted_iota(jnp.int32, (rows, rows), 1)
    packed = jnp.zeros((rows, rows), jnp.float32)
    scale = []
    local = []
    for which in range(2):
        highs = [found[which][0] for found in row_stats]
        high = functools.reduce(jnp.maximum, highs)
        scales = [jnp.exp(h - high) for h in highs]
        total = sum(s * found[which][1] for s, found in zip(scales, row_stats))
        packed = jnp.where(lane == 2 * which, high, packed)
        packed = jnp.where(lane == 2 * which + 1, total, packed)
        scale.append(scales)
        local.append((high, total))
    row_send[...] = jnp.transpose(packed)[:8, :]
    row_out = remote(
        row_send, row_recv, row_send_sem.at[0], row_recv_sem.at[0], device(partner, 1 - core)
    )
    row_out.start()

    for copy in col_out:
        copy.wait_recv()
    highs, sums = [], []
    for d in range(SQUARE):
        for e in range(2):
            slot = 2 * d + e
            value = col_stats[slot]
            order = [SQUARE * w + (k ^ d) for w in range(2) for k in range(SQUARE)]
            if d:
                highs.append(jnp.concatenate([value[k : k + 1] for k in order], axis=0))
                sums.append(jnp.concatenate([value[8 + k : 9 + k] for k in order], axis=0))
            else:
                highs.append(value[:8])
                sums.append(value[8:])
    column_high = functools.reduce(jnp.maximum, highs)
    column_total = sum(s * jnp.exp(h - column_high) for h, s in zip(highs, sums))
    column_factor = 0.5 * jnp.exp(highs[0] - column_high) / column_total

    row_out.wait_recv()
    other = jnp.transpose(jnp.concatenate([row_recv[...]] * (rows // 8), axis=0))
    row_factor = []
    for which in range(2):
        high, total = local[which]
        other_high = other[:, 2 * which : 2 * which + 1]
        other_total = other[:, 2 * which + 1 : 2 * which + 2]
        top = jnp.maximum(high, other_high)
        everything = total * jnp.exp(high - top) + other_total * jnp.exp(other_high - top)
        common = 0.5 * jnp.exp(high - top) / everything
        row_factor.append([common * s for s in scale[which]])

    share = None
    for d in range(SQUARE):
        weights = (
            er_s[d] * row_factor[0][d] - er_t[d] * row_factor[1][d]
        ) + (
            ec_s[d] * column_factor[d : d + 1] - ec_t[d] * column_factor[SQUARE + d : SQUARE + d + 1]
        )
        product = jnp.dot(
            weights.astype(jnp.bfloat16), txt_s[d], preferred_element_type=jnp.float32
        )
        share = product if share is None else share + product

    a_out = remote(part_a, part_a, a_send.at[0], a_recv.at[0], sibling)
    b_out = []
    for h in range(2):
        at = pl.ds(h * half, half)
        b_out.append(
            remote(part_c.at[at], part_b.at[at], b_send.at[h], b_recv.at[0], device(partner, h))
        )

    @pl.when(core == 0)
    def _():
        part_a[...] = share
        a_out.start()

    @pl.when(core == 1)
    def _():
        part_c[...] = share
        for copy in b_out:
            copy.start()

    remote(part_b.at[mine], part_b.at[mine], b_send.at[0], b_recv.at[0], sibling).wait_recv()
    b_forward = remote(part_b.at[mine], part_b.at[mine], b_send.at[2], b_recv.at[1], sibling)
    b_forward.start()

    @pl.when(core == 1)
    def _():
        a_out.wait_recv()

    remote(part_b.at[theirs], part_b.at[theirs], b_send.at[2], b_recv.at[1], sibling).wait_recv()
    out_ref[...] = part_a[...] + part_b[...]

    for copy in img_out + text_out[1] + text_out[2] + text_out[3] + col_out:
        copy.wait_send()
    for d in range(1, SQUARE):
        for copy in forward[d]:
            copy.wait_send()
    row_out.wait_send()
    b_forward.wait_send()

    @pl.when(core == 0)
    def _():
        a_out.wait_send()

    @pl.when(core == 1)
    def _():
        for copy in b_out:
            copy.wait_send()


def eight_chips(img_student, txt_student, img_teacher, txt_teacher):
    rows, narrow = img_student.shape
    wide = img_teacher.shape[1]
    dma = pltpu.SemaphoreType.DMA
    tiles = pltpu.VMEM((SQUARE, rows, rows), jnp.float32)
    partial = pltpu.VMEM((rows, narrow), jnp.float32)
    return pl.pallas_call(
        exchange_kernel,
        out_shape=jax.ShapeDtypeStruct((rows, narrow), jnp.float32),
        in_specs=[pl.BlockSpec(memory_space=pl.ANY)] * 4,
        out_specs=pl.BlockSpec(memory_space=pltpu.VMEM),
        scratch_shapes=[
            pltpu.VMEM((SQUARE, rows, narrow), jnp.bfloat16),
            pltpu.VMEM((SQUARE, rows, wide), jnp.bfloat16),
            pltpu.VMEM((rows, narrow), jnp.bfloat16),
            pltpu.VMEM((rows, wide), jnp.bfloat16),
            tiles, tiles, tiles, tiles,
            pltpu.VMEM((2 * SQUARE, 16, rows), jnp.float32),
            pltpu.VMEM((8, rows), jnp.float32),
            pltpu.VMEM((8, rows), jnp.float32),
            partial, partial, partial,
            dma((4,)),
            dma((2, SQUARE)), dma((2, SQUARE)), dma((2, SQUARE)), dma((2, SQUARE)),
            dma((2,)), dma((2, 2)),
            dma((2 * SQUARE,)), dma((2 * SQUARE,)), dma((1,)), dma((1,)),
            dma((1,)), dma((1,)), dma((3,)), dma((2,)),
        ],
        compiler_params=pltpu.CompilerParams(
            collective_id=0, has_side_effects=True, vmem_limit_bytes=32 * 1024 * 1024
        ),
        cost_estimate=pl.CostEstimate(
            flops=2 * rows * SQUARE * rows * (2 * narrow + wide),
            bytes_accessed=8 * rows * (narrow + wide),
            transcendentals=4 * SQUARE * rows * rows,
        ),
    )(img_student, txt_student, img_teacher, txt_teacher)


def solution(mesh):
    placed = P(("parts", "group"), None)

    def per_device(img_student, txt_student, img_teacher, txt_teacher):
        fits = (
            mesh.shape["group"] == 8
            and mesh.shape["blk"] == 2
            and img_student.shape[0] == 128
            and txt_student.shape[0] == 128
        )
        run = eight_chips if fits else general
        return run(img_student, txt_student, img_teacher, txt_teacher)

    return jax.shard_map(
        per_device,
        mesh=mesh,
        in_specs=(placed,) * 4,
        out_specs=placed,
        check_vma=False,
    )
```

```python
import functools

import jax
import jax.numpy as jnp
from jax import lax
from jax.experimental import pallas as pl
from jax.experimental.pallas import tpu as pltpu
from jax.sharding import PartitionSpec as P


def merged_2(value, axis, join):
    pieces = jax.tree.map(lambda part: lax.all_gather(part, axis), value)
    head = jax.tree.map(lambda part: part[0], pieces)
    tail = jax.tree.map(lambda part: part[1:], pieces)
    so_far, _ = lax.scan(lambda so_far, piece: (join(so_far, piece), None), head, tail)
    return so_far


def combine(earlier, later):
    merged = []
    for which in (0, 2):
        highest = jnp.maximum(earlier[which], later[which])
        total = earlier[which + 1] * jnp.exp(earlier[which] - highest) + later[which + 1] * jnp.exp(
            later[which] - highest
        )
        merged.append(highest)
        merged.append(total)
    return tuple(merged)


def general(img_student, txt_student, img_teacher, txt_teacher):
    half_rows = img_student.shape[0] // 2
    side = lax.axis_index("blk")
    begin = side * half_rows
    text_student_own = lax.dynamic_slice_in_dim(txt_student, begin, half_rows, 0)
    text_teacher_own = lax.dynamic_slice_in_dim(txt_teacher, begin, half_rows, 0)
    contract = (((1,), (1,)), ((), ()))
    text_student, text_teacher = (
        lax.all_gather(text_student_own, "group", axis=0, tiled=True),
        lax.all_gather(text_teacher_own, "group", axis=0, tiled=True),
    )
    student = lax.dot_general(
        img_student, text_student, contract, preferred_element_type=jnp.float32
    )
    teacher = lax.dot_general(
        img_teacher, text_teacher, contract, preferred_element_type=jnp.float32
    )
    row_student_high = jnp.max(student, axis=1)
    row_teacher_high = jnp.max(teacher, axis=1)
    row_stats = (
        row_student_high,
        jnp.sum(jnp.exp(student - row_student_high[:, None]), axis=1),
        row_teacher_high,
        jnp.sum(jnp.exp(teacher - row_teacher_high[:, None]), axis=1),
    )
    row_all = merged_2(row_stats, "blk", combine)
    row_student = (row_all[0] + jnp.log(row_all[1]))[:, None]
    row_teacher = (row_all[2] + jnp.log(row_all[3]))[:, None]
    column_student_high = jnp.max(student, axis=0)
    column_teacher_high = jnp.max(teacher, axis=0)
    column_stats = (
        column_student_high,
        jnp.sum(jnp.exp(student - column_student_high[None, :]), axis=0),
        column_teacher_high,
        jnp.sum(jnp.exp(teacher - column_teacher_high[None, :]), axis=0),
    )
    totals = merged_2(column_stats, "group", combine)
    column_student = (totals[0] + jnp.log(totals[1]))[None, :]
    column_teacher = (totals[2] + jnp.log(totals[3]))[None, :]
    row_part = jnp.exp(student - row_student) - jnp.exp(teacher - row_teacher)
    column_part = jnp.exp(student - column_student) - jnp.exp(teacher - column_teacher)
    weights = (0.5 * (row_part + column_part)).astype(jnp.bfloat16)
    partial_image = jnp.dot(weights, text_student, preferred_element_type=jnp.float32)
    return lax.psum(partial_image, "blk")


MESH = pl.DeviceIdType.MESH
SQUARE = 4


def exchange_kernel(
    img_s_hbm, txt_s_hbm, img_t_hbm, txt_t_hbm, out_ref,
    txt_s, txt_t, img_s, img_t,
    er_s, er_t, ec_s, ec_t,
    col_stats, row_send, row_recv, part_a, part_b, part_c,
    local_sem,
    txt_send, txt_recv, fwd_send, fwd_recv,
    img_send, img_recv,
    col_send, col_recv, row_send_sem, row_recv_sem,
    a_send, a_recv, b_send, b_recv,
):
    rows = img_s.shape[0]
    half = rows // 2
    group = lax.axis_index("group")
    core = lax.axis_index("blk")
    x = lax.rem(group, 2)
    b = lax.rem(group // 2, 2)
    a = group // 4

    def chip(d, other_half=0):
        return (
            lax.rem(a + other_half, 2) * 4
            + lax.rem(b + d // 2, 2) * 2
            + lax.rem(x + d % 2, 2)
        )

    def device(chip_index, core_index):
        return {"blk": core_index, "group": chip_index}

    sibling = device(group, 1 - core)
    partner = chip(0, 1)

    def remote(src, dst, send, recv, target):
        return pltpu.make_async_remote_copy(
            src_ref=src, dst_ref=dst, send_sem=send, recv_sem=recv,
            device_id=target, device_id_type=MESH,
        )

    mine = pl.ds(pl.multiple_of(core * half, half), half)
    theirs = pl.ds(pl.multiple_of((1 - core) * half, half), half)

    own = [
        pltpu.make_async_copy(txt_s_hbm, txt_s.at[0], local_sem.at[0]),
        pltpu.make_async_copy(txt_t_hbm, txt_t.at[0], local_sem.at[1]),
    ]
    own_img = [
        pltpu.make_async_copy(img_s_hbm, img_s, local_sem.at[2]),
        pltpu.make_async_copy(img_t_hbm, img_t, local_sem.at[3]),
    ]
    for copy in own:
        copy.start()

    @pl.when(core == 0)
    def _():
        for copy in own_img:
            copy.start()

    barrier = pltpu.get_barrier_semaphore()
    greeted = [sibling, device(partner, core), device(partner, 1 - core)]
    for d in range(1, SQUARE):
        greeted += [device(chip(d), core), device(chip(d), 1 - core)]
    for target in greeted:
        pl.semaphore_signal(barrier, inc=1, device_id=target, device_id_type=MESH)
    pl.semaphore_wait(barrier, len(greeted))

    img_out = [
        remote(img_s_hbm.at[mine], img_s.at[mine], img_send.at[0], img_recv.at[0, core], device(partner, 1)),
        remote(img_t_hbm.at[mine], img_t.at[mine], img_send.at[1], img_recv.at[1, core], device(partner, 1)),
    ]
    text_out = {}
    for d in range(1, SQUARE):
        text_out[d] = [
            remote(txt_s_hbm.at[mine], txt_s.at[d, mine], txt_send.at[0, d], txt_recv.at[0, d], device(chip(d), core)),
            remote(txt_t_hbm.at[mine], txt_t.at[d, mine], txt_send.at[1, d], txt_recv.at[1, d], device(chip(d), core)),
        ]
    img_out[0].start()
    for copy in text_out[1] + text_out[2]:
        copy.start()
    img_out[1].start()
    for copy in text_out[3]:
        copy.start()

    forward = {}

    def pass_on(d):
        forward[d] = []
        for which, ref in ((0, txt_s), (1, txt_t)):
            text_out[d][which].wait_recv()
            copy = remote(
                ref.at[d, mine], ref.at[d, mine],
                fwd_send.at[which, d], fwd_recv.at[which, d], sibling,
            )
            copy.start()
            forward[d].append(copy)

    contract = (((1,), (1,)), ((), ()))
    row_stats = []

    def tile(d):
        if d == 0:
            for copy in own:
                copy.wait()
        else:
            for which, ref in ((0, txt_s), (1, txt_t)):
                remote(
                    ref.at[d, theirs], ref.at[d, theirs],
                    fwd_send.at[which, d], fwd_recv.at[which, d], sibling,
                ).wait_recv()
        found = []
        for which, (img, txt, er, ec) in enumerate(
            ((img_s, txt_s, er_s, ec_s), (img_t, txt_t, er_t, ec_t))
        ):
            logits = lax.dot_general(
                img[...], txt[d], contract, preferred_element_type=jnp.float32
            )
            row_high = jnp.max(logits, axis=1, keepdims=True)
            row_exp = jnp.exp(logits - row_high)
            er[d] = row_exp
            found.append((row_high, jnp.sum(row_exp, axis=1, keepdims=True)))
            column_high = jnp.max(logits, axis=0, keepdims=True)
            column_exp = jnp.exp(logits - column_high)
            ec[d] = column_exp
            at = which * SQUARE + d
            col_stats[0, at : at + 1, :] = column_high
            col_stats[0, 8 + at : 9 + at, :] = jnp.sum(column_exp, axis=0, keepdims=True)
        row_stats.append(found)

    pass_on(1)

    @pl.when(core == 0)
    def _():
        for copy in own_img:
            copy.wait()

    @pl.when(core == 1)
    def _():
        for h in range(2):
            at = pl.ds(h * half, half)
            for which, ref in ((0, img_s), (1, img_t)):
                remote(
                    ref.at[at], ref.at[at], img_send.at[which], img_recv.at[which, h], device(partner, 1)
                ).wait_recv()

    tile(0)
    pass_on(2)
    tile(1)
    pass_on(3)
    tile(2)
    tile(3)

    col_out = []
    for d in range(SQUARE):
        for e in range(2):
            slot = 2 * d + e
            if slot:
                target = device(chip(d), core if e == 0 else 1 - core)
                copy = remote(
                    col_stats.at[0], col_stats.at[slot], col_send.at[slot], col_recv.at[slot], target
                )
                copy.start()
                col_out.append(copy)

    lane = lax.broadcasted_iota(jnp.int32, (rows, rows), 1)
    packed = jnp.zeros((rows, rows), jnp.float32)
    scale = []
    local = []
    for which in range(2):
        highs = [found[which][0] for found in row_stats]
        high = functools.reduce(jnp.maximum, highs)
        scales = [jnp.exp(h - high) for h in highs]
        total = sum(s * found[which][1] for s, found in zip(scales, row_stats))
        packed = jnp.where(lane == 2 * which, high, packed)
        packed = jnp.where(lane == 2 * which + 1, total, packed)
        scale.append(scales)
        local.append((high, total))
    row_send[...] = jnp.transpose(packed)[:8, :]
    row_out = remote(
        row_send, row_recv, row_send_sem.at[0], row_recv_sem.at[0], device(partner, 1 - core)
    )
    row_out.start()

    for copy in col_out:
        copy.wait_recv()
    highs, sums = [], []
    for d in range(SQUARE):
        for e in range(2):
            slot = 2 * d + e
            value = col_stats[slot]
            order = [SQUARE * w + (k ^ d) for w in range(2) for k in range(SQUARE)]
            if d:
                highs.append(jnp.concatenate([value[k : k + 1] for k in order], axis=0))
                sums.append(jnp.concatenate([value[8 + k : 9 + k] for k in order], axis=0))
            else:
                highs.append(value[:8])
                sums.append(value[8:])
    column_high = functools.reduce(jnp.maximum, highs)
    column_total = sum(s * jnp.exp(h - column_high) for h, s in zip(highs, sums))
    column_factor = 0.5 * jnp.exp(highs[0] - column_high) / column_total

    row_out.wait_recv()
    other = jnp.transpose(jnp.concatenate([row_recv[...]] * (rows // 8), axis=0))
    row_factor = []
    for which in range(2):
        high, total = local[which]
        other_high = other[:, 2 * which : 2 * which + 1]
        other_total = other[:, 2 * which + 1 : 2 * which + 2]
        top = jnp.maximum(high, other_high)
        everything = total * jnp.exp(high - top) + other_total * jnp.exp(other_high - top)
        common = 0.5 * jnp.exp(high - top) / everything
        row_factor.append([common * s for s in scale[which]])

    share = None
    for d in range(SQUARE):
        weights = (
            er_s[d] * row_factor[0][d] - er_t[d] * row_factor[1][d]
        ) + (
            ec_s[d] * column_factor[d : d + 1] - ec_t[d] * column_factor[SQUARE + d : SQUARE + d + 1]
        )
        product = jnp.dot(
            weights.astype(jnp.bfloat16), txt_s[d], preferred_element_type=jnp.float32
        )
        share = product if share is None else share + product

    a_out = remote(part_a, part_a, a_send.at[0], a_recv.at[0], sibling)
    b_out = []
    for h in range(2):
        at = pl.ds(h * half, half)
        b_out.append(
            remote(part_c.at[at], part_b.at[at], b_send.at[h], b_recv.at[0], device(partner, h))
        )

    @pl.when(core == 0)
    def _():
        part_a[...] = share
        a_out.start()

    @pl.when(core == 1)
    def _():
        part_c[...] = share
        for copy in b_out:
            copy.start()

    remote(part_b.at[mine], part_b.at[mine], b_send.at[0], b_recv.at[0], sibling).wait_recv()
    b_forward = remote(part_b.at[mine], part_b.at[mine], b_send.at[2], b_recv.at[1], sibling)
    b_forward.start()

    @pl.when(core == 1)
    def _():
        a_out.wait_recv()

    remote(part_b.at[theirs], part_b.at[theirs], b_send.at[2], b_recv.at[1], sibling).wait_recv()
    out_ref[...] = part_a[...] + part_b[...]

    for copy in img_out + text_out[1] + text_out[2] + text_out[3] + col_out:
        copy.wait_send()
    for d in range(1, SQUARE):
        for copy in forward[d]:
            copy.wait_send()
    row_out.wait_send()
    b_forward.wait_send()

    @pl.when(core == 0)
    def _():
        a_out.wait_send()

    @pl.when(core == 1)
    def _():
        for copy in b_out:
            copy.wait_send()


def eight_chips(img_student, txt_student, img_teacher, txt_teacher):
    rows, narrow = img_student.shape
    wide = img_teacher.shape[1]
    dma = pltpu.SemaphoreType.DMA
    tiles = pltpu.VMEM((SQUARE, rows, rows), jnp.float32)
    partial = pltpu.VMEM((rows, narrow), jnp.float32)
    return pl.pallas_call(
        exchange_kernel,
        out_shape=jax.ShapeDtypeStruct((rows, narrow), jnp.float32),
        in_specs=[pl.BlockSpec(memory_space=pltpu.HBM)] * 4,
        out_specs=pl.BlockSpec(memory_space=pltpu.VMEM),
        scratch_shapes=[
            pltpu.VMEM((SQUARE, rows, narrow), jnp.bfloat16),
            pltpu.VMEM((SQUARE, rows, wide), jnp.bfloat16),
            pltpu.VMEM((rows, narrow), jnp.bfloat16),
            pltpu.VMEM((rows, wide), jnp.bfloat16),
            tiles, tiles, tiles, tiles,
            pltpu.VMEM((2 * SQUARE, 16, rows), jnp.float32),
            pltpu.VMEM((8, rows), jnp.float32),
            pltpu.VMEM((8, rows), jnp.float32),
            partial, partial, partial,
            dma((4,)),
            dma((2, SQUARE)), dma((2, SQUARE)), dma((2, SQUARE)), dma((2, SQUARE)),
            dma((2,)), dma((2, 2)),
            dma((2 * SQUARE,)), dma((2 * SQUARE,)), dma((1,)), dma((1,)),
            dma((1,)), dma((1,)), dma((3,)), dma((2,)),
        ],
        compiler_params=pltpu.CompilerParams(
            collective_id=0, has_side_effects=True, vmem_limit_bytes=60 * 1024 * 1024
        ),
        cost_estimate=pl.CostEstimate(
            flops=2 * rows * SQUARE * rows * (2 * narrow + wide),
            bytes_accessed=8 * rows * (narrow + wide),
            transcendentals=4 * SQUARE * rows * rows,
        ),
    )(img_student, txt_student, img_teacher, txt_teacher)


def solution(mesh):
    placed = P(("parts", "group"), None)

    def per_device(img_student, txt_student, img_teacher, txt_teacher):
        fits = (
            mesh.shape["group"] == 8
            and mesh.shape["blk"] == 2
            and img_student.shape[0] == 128
            and txt_student.shape[0] == 128
        )
        run = eight_chips if fits else general
        return run(img_student, txt_student, img_teacher, txt_teacher)

    return jax.shard_map(
        per_device,
        mesh=mesh,
        in_specs=(placed,) * 4,
        out_specs=placed,
        check_vma=False,
    )
```

```python
import functools

import jax
import jax.numpy as jnp
from jax import lax
from jax.experimental import pallas as pl
from jax.experimental.pallas import tpu as pltpu
from jax.sharding import PartitionSpec as P


def merged_2(value, axis, join):
    pieces = jax.tree.map(lambda part: lax.all_gather(part, axis), value)
    head = jax.tree.map(lambda part: part[0], pieces)
    tail = jax.tree.map(lambda part: part[1:], pieces)
    so_far, _ = lax.scan(lambda so_far, piece: (join(so_far, piece), None), head, tail)
    return so_far


def combine(earlier, later):
    merged = []
    for which in (0, 2):
        highest = jnp.maximum(earlier[which], later[which])
        total = earlier[which + 1] * jnp.exp(earlier[which] - highest) + later[which + 1] * jnp.exp(
            later[which] - highest
        )
        merged.append(highest)
        merged.append(total)
    return tuple(merged)


def general(img_student, txt_student, img_teacher, txt_teacher):
    half_rows = img_student.shape[0] // 2
    side = lax.axis_index("blk")
    begin = side * half_rows
    text_student_own = lax.dynamic_slice_in_dim(txt_student, begin, half_rows, 0)
    text_teacher_own = lax.dynamic_slice_in_dim(txt_teacher, begin, half_rows, 0)
    contract = (((1,), (1,)), ((), ()))
    text_student, text_teacher = (
        lax.all_gather(text_student_own, "group", axis=0, tiled=True),
        lax.all_gather(text_teacher_own, "group", axis=0, tiled=True),
    )
    student = lax.dot_general(
        img_student, text_student, contract, preferred_element_type=jnp.float32
    )
    teacher = lax.dot_general(
        img_teacher, text_teacher, contract, preferred_element_type=jnp.float32
    )
    row_student_high = jnp.max(student, axis=1)
    row_teacher_high = jnp.max(teacher, axis=1)
    row_stats = (
        row_student_high,
        jnp.sum(jnp.exp(student - row_student_high[:, None]), axis=1),
        row_teacher_high,
        jnp.sum(jnp.exp(teacher - row_teacher_high[:, None]), axis=1),
    )
    row_all = merged_2(row_stats, "blk", combine)
    row_student = (row_all[0] + jnp.log(row_all[1]))[:, None]
    row_teacher = (row_all[2] + jnp.log(row_all[3]))[:, None]
    column_student_high = jnp.max(student, axis=0)
    column_teacher_high = jnp.max(teacher, axis=0)
    column_stats = (
        column_student_high,
        jnp.sum(jnp.exp(student - column_student_high[None, :]), axis=0),
        column_teacher_high,
        jnp.sum(jnp.exp(teacher - column_teacher_high[None, :]), axis=0),
    )
    totals = merged_2(column_stats, "group", combine)
    column_student = (totals[0] + jnp.log(totals[1]))[None, :]
    column_teacher = (totals[2] + jnp.log(totals[3]))[None, :]
    row_part = jnp.exp(student - row_student) - jnp.exp(teacher - row_teacher)
    column_part = jnp.exp(student - column_student) - jnp.exp(teacher - column_teacher)
    weights = (0.5 * (row_part + column_part)).astype(jnp.bfloat16)
    partial_image = jnp.dot(weights, text_student, preferred_element_type=jnp.float32)
    return lax.psum(partial_image, "blk")


MESH = pl.DeviceIdType.MESH
SQUARE = 4


def exchange_kernel(
    img_s_hbm, txt_s_hbm, img_t_hbm, txt_t_hbm, out_ref,
    txt_s, txt_t, img_s, img_t,
    er_s, er_t, ec_s, ec_t,
    col_stats, row_send, row_recv, part_a, part_b, part_c,
    local_sem,
    txt_send, txt_recv, fwd_send, fwd_recv,
    img_send, img_recv,
    col_send, col_recv, row_send_sem, row_recv_sem,
    a_send, a_recv, b_send, b_recv,
):
    rows = img_s.shape[0]
    half = rows // 2
    group = lax.axis_index("group")
    core = lax.axis_index("blk")
    x = lax.rem(group, 2)
    b = lax.rem(group // 2, 2)
    a = group // 4

    def chip(d, other_half=0):
        return (
            lax.rem(a + other_half, 2) * 4
            + lax.rem(b + d // 2, 2) * 2
            + lax.rem(x + d % 2, 2)
        )

    def device(chip_index, core_index):
        return {"blk": core_index, "group": chip_index}

    sibling = device(group, 1 - core)
    partner = chip(0, 1)

    def remote(src, dst, send, recv, target):
        return pltpu.make_async_remote_copy(
            src_ref=src, dst_ref=dst, send_sem=send, recv_sem=recv,
            device_id=target, device_id_type=MESH,
        )

    mine = pl.ds(pl.multiple_of(core * half, half), half)
    theirs = pl.ds(pl.multiple_of((1 - core) * half, half), half)

    own = [
        pltpu.make_async_copy(txt_s_hbm, txt_s.at[0], local_sem.at[0]),
        pltpu.make_async_copy(txt_t_hbm, txt_t.at[0], local_sem.at[1]),
    ]
    own_img = [
        pltpu.make_async_copy(img_s_hbm, img_s, local_sem.at[2]),
        pltpu.make_async_copy(img_t_hbm, img_t, local_sem.at[3]),
    ]
    for copy in own:
        copy.start()

    @pl.when(core == 0)
    def _():
        for copy in own_img:
            copy.start()

    barrier = pltpu.get_barrier_semaphore()
    greeted = [sibling, device(partner, core), device(partner, 1 - core)]
    for d in range(1, SQUARE):
        greeted += [device(chip(d), core), device(chip(d), 1 - core)]
    for target in greeted:
        pl.semaphore_signal(barrier, inc=1, device_id=target, device_id_type=MESH)
    pl.semaphore_wait(barrier, len(greeted))

    img_out = [
        remote(img_s_hbm.at[mine], img_s.at[mine], img_send.at[0], img_recv.at[0, core], device(partner, 1)),
        remote(img_t_hbm.at[mine], img_t.at[mine], img_send.at[1], img_recv.at[1, core], device(partner, 1)),
    ]
    text_out = {}
    for d in range(1, SQUARE):
        text_out[d] = [
            remote(txt_s_hbm.at[mine], txt_s.at[d, mine], txt_send.at[0, d], txt_recv.at[0, d], device(chip(d), core)),
            remote(txt_t_hbm.at[mine], txt_t.at[d, mine], txt_send.at[1, d], txt_recv.at[1, d], device(chip(d), core)),
        ]
    for copy in text_out[3] + img_out + text_out[1] + text_out[2]:
        copy.start()

    forward = {}

    def pass_on(d):
        forward[d] = []
        for which, ref in ((0, txt_s), (1, txt_t)):
            text_out[d][which].wait_recv()
            copy = remote(
                ref.at[d, mine], ref.at[d, mine],
                fwd_send.at[which, d], fwd_recv.at[which, d], sibling,
            )
            copy.start()
            forward[d].append(copy)

    contract = (((1,), (1,)), ((), ()))
    row_stats = []

    def tile(d):
        if d == 0:
            for copy in own:
                copy.wait()
        else:
            for which, ref in ((0, txt_s), (1, txt_t)):
                remote(
                    ref.at[d, theirs], ref.at[d, theirs],
                    fwd_send.at[which, d], fwd_recv.at[which, d], sibling,
                ).wait_recv()
        found = []
        for which, (img, txt, er, ec) in enumerate(
            ((img_s, txt_s, er_s, ec_s), (img_t, txt_t, er_t, ec_t))
        ):
            logits = lax.dot_general(
                img[...], txt[d], contract, preferred_element_type=jnp.float32
            )
            row_high = jnp.max(logits, axis=1, keepdims=True)
            row_exp = jnp.exp(logits - row_high)
            er[d] = row_exp
            found.append((row_high, jnp.sum(row_exp, axis=1, keepdims=True)))
            column_high = jnp.max(logits, axis=0, keepdims=True)
            column_exp = jnp.exp(logits - column_high)
            ec[d] = column_exp
            at = which * SQUARE + d
            col_stats[0, at : at + 1, :] = column_high
            col_stats[0, 8 + at : 9 + at, :] = jnp.sum(column_exp, axis=0, keepdims=True)
        row_stats.append(found)

    pass_on(1)

    @pl.when(core == 0)
    def _():
        for copy in own_img:
            copy.wait()

    @pl.when(core == 1)
    def _():
        for h in range(2):
            at = pl.ds(h * half, half)
            for which, ref in ((0, img_s), (1, img_t)):
                remote(
                    ref.at[at], ref.at[at], img_send.at[which], img_recv.at[which, h], device(partner, 1)
                ).wait_recv()

    tile(0)
    pass_on(2)
    tile(1)
    pass_on(3)
    tile(2)
    tile(3)

    col_out = []
    for d in range(SQUARE):
        for e in range(2):
            slot = 2 * d + e
            if slot:
                target = device(chip(d), core if e == 0 else 1 - core)
                copy = remote(
                    col_stats.at[0], col_stats.at[slot], col_send.at[slot], col_recv.at[slot], target
                )
                copy.start()
                col_out.append(copy)

    lane = lax.broadcasted_iota(jnp.int32, (rows, rows), 1)
    packed = jnp.zeros((rows, rows), jnp.float32)
    scale = []
    local = []
    for which in range(2):
        highs = [found[which][0] for found in row_stats]
        high = functools.reduce(jnp.maximum, highs)
        scales = [jnp.exp(h - high) for h in highs]
        total = sum(s * found[which][1] for s, found in zip(scales, row_stats))
        packed = jnp.where(lane == 2 * which, high, packed)
        packed = jnp.where(lane == 2 * which + 1, total, packed)
        scale.append(scales)
        local.append((high, total))
    row_send[...] = jnp.transpose(packed)[:8, :]
    row_out = remote(
        row_send, row_recv, row_send_sem.at[0], row_recv_sem.at[0], device(partner, 1 - core)
    )
    row_out.start()

    for copy in col_out:
        copy.wait_recv()
    highs, sums = [], []
    for d in range(SQUARE):
        for e in range(2):
            slot = 2 * d + e
            value = col_stats[slot]
            order = [SQUARE * w + (k ^ d) for w in range(2) for k in range(SQUARE)]
            if d:
                highs.append(jnp.concatenate([value[k : k + 1] for k in order], axis=0))
                sums.append(jnp.concatenate([value[8 + k : 9 + k] for k in order], axis=0))
            else:
                highs.append(value[:8])
                sums.append(value[8:])
    column_high = functools.reduce(jnp.maximum, highs)
    column_total = sum(s * jnp.exp(h - column_high) for h, s in zip(highs, sums))
    column_factor = 0.5 * jnp.exp(highs[0] - column_high) / column_total

    row_out.wait_recv()
    other = jnp.transpose(jnp.concatenate([row_recv[...]] * (rows // 8), axis=0))
    row_factor = []
    for which in range(2):
        high, total = local[which]
        other_high = other[:, 2 * which : 2 * which + 1]
        other_total = other[:, 2 * which + 1 : 2 * which + 2]
        top = jnp.maximum(high, other_high)
        everything = total * jnp.exp(high - top) + other_total * jnp.exp(other_high - top)
        common = 0.5 * jnp.exp(high - top) / everything
        row_factor.append([common * s for s in scale[which]])

    share = None
    for d in range(SQUARE):
        weights = (
            er_s[d] * row_factor[0][d] - er_t[d] * row_factor[1][d]
        ) + (
            ec_s[d] * column_factor[d : d + 1] - ec_t[d] * column_factor[SQUARE + d : SQUARE + d + 1]
        )
        product = jnp.dot(
            weights.astype(jnp.bfloat16), txt_s[d], preferred_element_type=jnp.float32
        )
        share = product if share is None else share + product

    a_out = remote(part_a, part_a, a_send.at[0], a_recv.at[0], sibling)
    b_out = []
    for h in range(2):
        at = pl.ds(h * half, half)
        b_out.append(
            remote(part_c.at[at], part_b.at[at], b_send.at[h], b_recv.at[0], device(partner, h))
        )

    @pl.when(core == 0)
    def _():
        part_a[...] = share
        a_out.start()

    @pl.when(core == 1)
    def _():
        part_c[...] = share.astype(part_c.dtype)
        for copy in b_out:
            copy.start()

    remote(part_b.at[mine], part_b.at[mine], b_send.at[0], b_recv.at[0], sibling).wait_recv()
    b_forward = remote(part_b.at[mine], part_b.at[mine], b_send.at[2], b_recv.at[1], sibling)
    b_forward.start()

    @pl.when(core == 1)
    def _():
        a_out.wait_recv()

    remote(part_b.at[theirs], part_b.at[theirs], b_send.at[2], b_recv.at[1], sibling).wait_recv()
    out_ref[...] = part_a[...] + part_b[...].astype(jnp.float32)

    for copy in img_out + text_out[1] + text_out[2] + text_out[3] + col_out:
        copy.wait_send()
    for d in range(1, SQUARE):
        for copy in forward[d]:
            copy.wait_send()
    row_out.wait_send()
    b_forward.wait_send()

    @pl.when(core == 0)
    def _():
        a_out.wait_send()

    @pl.when(core == 1)
    def _():
        for copy in b_out:
            copy.wait_send()


def eight_chips(img_student, txt_student, img_teacher, txt_teacher):
    rows, narrow = img_student.shape
    wide = img_teacher.shape[1]
    dma = pltpu.SemaphoreType.DMA
    tiles = pltpu.VMEM((SQUARE, rows, rows), jnp.float32)
    partial = pltpu.VMEM((rows, narrow), jnp.float32)
    travelling = pltpu.VMEM((rows, narrow), jnp.bfloat16)
    return pl.pallas_call(
        exchange_kernel,
        out_shape=pltpu.VMEM((rows, narrow), jnp.float32),
        in_specs=[pl.BlockSpec(memory_space=pltpu.HBM)] * 4,
        out_specs=pl.BlockSpec(memory_space=pltpu.VMEM),
        scratch_shapes=[
            pltpu.VMEM((SQUARE, rows, narrow), jnp.bfloat16),
            pltpu.VMEM((SQUARE, rows, wide), jnp.bfloat16),
            pltpu.VMEM((rows, narrow), jnp.bfloat16),
            pltpu.VMEM((rows, wide), jnp.bfloat16),
            tiles, tiles, tiles, tiles,
            pltpu.VMEM((2 * SQUARE, 16, rows), jnp.float32),
            pltpu.VMEM((8, rows), jnp.float32),
            pltpu.VMEM((8, rows), jnp.float32),
            partial, travelling, travelling,
            dma((4,)),
            dma((2, SQUARE)), dma((2, SQUARE)), dma((2, SQUARE)), dma((2, SQUARE)),
            dma((2,)), dma((2, 2)),
            dma((2 * SQUARE,)), dma((2 * SQUARE,)), dma((1,)), dma((1,)),
            dma((1,)), dma((1,)), dma((3,)), dma((2,)),
        ],
        compiler_params=pltpu.CompilerParams(
            collective_id=0, has_side_effects=True, vmem_limit_bytes=60 * 1024 * 1024
        ),
        cost_estimate=pl.CostEstimate(
            flops=2 * rows * SQUARE * rows * (2 * narrow + wide),
            bytes_accessed=8 * rows * (narrow + wide),
            transcendentals=4 * SQUARE * rows * rows,
        ),
    )(img_student, txt_student, img_teacher, txt_teacher)


def solution(mesh):
    placed = P(("parts", "group"), None)

    def per_device(img_student, txt_student, img_teacher, txt_teacher):
        fits = (
            mesh.shape["group"] == 8
            and mesh.shape["blk"] == 2
            and img_student.shape[0] == 128
            and txt_student.shape[0] == 128
        )
        run = eight_chips if fits else general
        return run(img_student, txt_student, img_teacher, txt_teacher)

    return jax.shard_map(
        per_device,
        mesh=mesh,
        in_specs=(placed,) * 4,
        out_specs=placed,
        check_vma=False,
    )
```

```python
import functools

import jax
import jax.numpy as jnp
from jax import lax
from jax.experimental import pallas as pl
from jax.experimental.pallas import tpu as pltpu
from jax.sharding import PartitionSpec as P


def merged_2(value, axis, join):
    pieces = jax.tree.map(lambda part: lax.all_gather(part, axis), value)
    head = jax.tree.map(lambda part: part[0], pieces)
    tail = jax.tree.map(lambda part: part[1:], pieces)
    so_far, _ = lax.scan(lambda so_far, piece: (join(so_far, piece), None), head, tail)
    return so_far


def combine(earlier, later):
    merged = []
    for which in (0, 2):
        highest = jnp.maximum(earlier[which], later[which])
        total = earlier[which + 1] * jnp.exp(earlier[which] - highest) + later[which + 1] * jnp.exp(
            later[which] - highest
        )
        merged.append(highest)
        merged.append(total)
    return tuple(merged)


def general(img_student, txt_student, img_teacher, txt_teacher):
    half_rows = img_student.shape[0] // 2
    side = lax.axis_index("blk")
    begin = side * half_rows
    text_student_own = lax.dynamic_slice_in_dim(txt_student, begin, half_rows, 0)
    text_teacher_own = lax.dynamic_slice_in_dim(txt_teacher, begin, half_rows, 0)
    contract = (((1,), (1,)), ((), ()))
    text_student, text_teacher = (
        lax.all_gather(text_student_own, "group", axis=0, tiled=True),
        lax.all_gather(text_teacher_own, "group", axis=0, tiled=True),
    )
    student = lax.dot_general(
        img_student, text_student, contract, preferred_element_type=jnp.float32
    )
    teacher = lax.dot_general(
        img_teacher, text_teacher, contract, preferred_element_type=jnp.float32
    )
    row_student_high = jnp.max(student, axis=1)
    row_teacher_high = jnp.max(teacher, axis=1)
    row_stats = (
        row_student_high,
        jnp.sum(jnp.exp(student - row_student_high[:, None]), axis=1),
        row_teacher_high,
        jnp.sum(jnp.exp(teacher - row_teacher_high[:, None]), axis=1),
    )
    row_all = merged_2(row_stats, "blk", combine)
    row_student = (row_all[0] + jnp.log(row_all[1]))[:, None]
    row_teacher = (row_all[2] + jnp.log(row_all[3]))[:, None]
    column_student_high = jnp.max(student, axis=0)
    column_teacher_high = jnp.max(teacher, axis=0)
    column_stats = (
        column_student_high,
        jnp.sum(jnp.exp(student - column_student_high[None, :]), axis=0),
        column_teacher_high,
        jnp.sum(jnp.exp(teacher - column_teacher_high[None, :]), axis=0),
    )
    totals = merged_2(column_stats, "group", combine)
    column_student = (totals[0] + jnp.log(totals[1]))[None, :]
    column_teacher = (totals[2] + jnp.log(totals[3]))[None, :]
    row_part = jnp.exp(student - row_student) - jnp.exp(teacher - row_teacher)
    column_part = jnp.exp(student - column_student) - jnp.exp(teacher - column_teacher)
    weights = (0.5 * (row_part + column_part)).astype(jnp.bfloat16)
    partial_image = jnp.dot(weights, text_student, preferred_element_type=jnp.float32)
    return lax.psum(partial_image, "blk")


MESH = pl.DeviceIdType.MESH
SQUARE = 4


def exchange_kernel(
    img_s_hbm, txt_s_hbm, img_t_hbm, txt_t_hbm, out_ref,
    txt_s, txt_t, img_s, img_t,
    er_s, er_t, ec_s, ec_t,
    col_stats, row_send, row_recv, part_a, part_b, part_c,
    local_sem,
    txt_send, txt_recv, fwd_send, fwd_recv,
    img_send, img_recv,
    col_send, col_recv, row_send_sem, row_recv_sem,
    a_send, a_recv, b_send, b_recv,
):
    rows = img_s.shape[0]
    half = rows // 2
    group = lax.axis_index("group")
    core = lax.axis_index("blk")
    x = lax.rem(group, 2)
    b = lax.rem(group // 2, 2)
    a = group // 4

    def chip(d, other_half=0):
        return (
            lax.rem(a + other_half, 2) * 4
            + lax.rem(b + d // 2, 2) * 2
            + lax.rem(x + d % 2, 2)
        )

    def device(chip_index, core_index):
        return {"blk": core_index, "group": chip_index}

    sibling = device(group, 1 - core)
    partner = chip(0, 1)

    def remote(src, dst, send, recv, target):
        return pltpu.make_async_remote_copy(
            src_ref=src, dst_ref=dst, send_sem=send, recv_sem=recv,
            device_id=target, device_id_type=MESH,
        )

    mine = pl.ds(pl.multiple_of(core * half, half), half)
    theirs = pl.ds(pl.multiple_of((1 - core) * half, half), half)

    own = [
        pltpu.make_async_copy(txt_s_hbm, txt_s.at[0], local_sem.at[0]),
        pltpu.make_async_copy(txt_t_hbm, txt_t.at[0], local_sem.at[1]),
    ]
    own_img = [
        pltpu.make_async_copy(img_s_hbm, img_s, local_sem.at[2]),
        pltpu.make_async_copy(img_t_hbm, img_t, local_sem.at[3]),
    ]
    for copy in own:
        copy.start()

    @pl.when(core == 0)
    def _():
        for copy in own_img:
            copy.start()

    barrier = pltpu.get_barrier_semaphore()
    greeted = [sibling, device(partner, core), device(partner, 1 - core)]
    for d in range(1, SQUARE):
        greeted += [device(chip(d), core), device(chip(d), 1 - core)]
    for target in greeted:
        pl.semaphore_signal(barrier, inc=1, device_id=target, device_id_type=MESH)
    pl.semaphore_wait(barrier, len(greeted))

    img_out = [
        remote(img_s_hbm.at[mine], img_s.at[mine], img_send.at[0], img_recv.at[0, core], device(partner, 1)),
        remote(img_t_hbm.at[mine], img_t.at[mine], img_send.at[1], img_recv.at[1, core], device(partner, 1)),
    ]
    text_out = {}
    for d in range(1, SQUARE):
        text_out[d] = [
            remote(txt_s_hbm.at[mine], txt_s.at[d, mine], txt_send.at[0, d], txt_recv.at[0, d], device(chip(d), core)),
        ]
    for d in (1, 2):
        text_out[d].append(
            remote(txt_t_hbm.at[mine], txt_t.at[d, mine], txt_send.at[1, d], txt_recv.at[1, d], device(chip(d), core))
        )
    text_out[3].append(remote(
        txt_t.at[2, mine], txt_t.at[3, mine], txt_send.at[1, 3], txt_recv.at[1, 3], device(chip(1), core)
    ))
    for copy in (
        [text_out[2][1], text_out[3][0]] + img_out + [text_out[1][1], text_out[1][0], text_out[2][0]]
    ):
        copy.start()

    forward = {}

    def pass_on(d, which):
        ref = (txt_s, txt_t)[which]
        text_out[d][which].wait_recv()
        if (d, which) == (2, 1):
            text_out[3][1].start()
        copy = remote(
            ref.at[d, mine], ref.at[d, mine],
            fwd_send.at[which, d], fwd_recv.at[which, d], sibling,
        )
        copy.start()
        forward[d, which] = copy

    contract = (((1,), (1,)), ((), ()))
    row_stats = []

    def tile(d):
        if d == 0:
            for copy in own:
                copy.wait()
        else:
            for which, ref in ((0, txt_s), (1, txt_t)):
                remote(
                    ref.at[d, theirs], ref.at[d, theirs],
                    fwd_send.at[which, d], fwd_recv.at[which, d], sibling,
                ).wait_recv()
        found = []
        for which, (img, txt, er, ec) in enumerate(
            ((img_s, txt_s, er_s, ec_s), (img_t, txt_t, er_t, ec_t))
        ):
            logits = lax.dot_general(
                img[...], txt[d], contract, preferred_element_type=jnp.float32
            )
            row_high = jnp.max(logits, axis=1, keepdims=True)
            row_exp = jnp.exp(logits - row_high)
            er[d] = row_exp
            found.append((row_high, jnp.sum(row_exp, axis=1, keepdims=True)))
            column_high = jnp.max(logits, axis=0, keepdims=True)
            column_exp = jnp.exp(logits - column_high)
            ec[d] = column_exp
            at = which * SQUARE + d
            col_stats[0, at : at + 1, :] = column_high
            col_stats[0, 8 + at : 9 + at, :] = jnp.sum(column_exp, axis=0, keepdims=True)
        row_stats.append(found)

    pass_on(2, 1)
    pass_on(1, 1)
    pass_on(1, 0)
    pass_on(2, 0)

    @pl.when(core == 0)
    def _():
        for copy in own_img:
            copy.wait()

    @pl.when(core == 1)
    def _():
        for h in range(2):
            at = pl.ds(h * half, half)
            for which, ref in ((0, img_s), (1, img_t)):
                remote(
                    ref.at[at], ref.at[at], img_send.at[which], img_recv.at[which, h], device(partner, 1)
                ).wait_recv()

    tile(0)
    pass_on(3, 0)
    pass_on(3, 1)
    tile(1)
    tile(2)
    tile(3)

    col_out = []
    for d in range(SQUARE):
        for e in range(2):
            slot = 2 * d + e
            if slot:
                target = device(chip(d), core if e == 0 else 1 - core)
                copy = remote(
                    col_stats.at[0], col_stats.at[slot], col_send.at[slot], col_recv.at[slot], target
                )
                copy.start()
                col_out.append(copy)

    lane = lax.broadcasted_iota(jnp.int32, (rows, rows), 1)
    packed = jnp.zeros((rows, rows), jnp.float32)
    scale = []
    local = []
    for which in range(2):
        highs = [found[which][0] for found in row_stats]
        high = functools.reduce(jnp.maximum, highs)
        scales = [jnp.exp(h - high) for h in highs]
        total = sum(s * found[which][1] for s, found in zip(scales, row_stats))
        packed = jnp.where(lane == 2 * which, high, packed)
        packed = jnp.where(lane == 2 * which + 1, total, packed)
        scale.append(scales)
        local.append((high, total))
    row_send[...] = jnp.transpose(packed)[:8, :]
    row_out = remote(
        row_send, row_recv, row_send_sem.at[0], row_recv_sem.at[0], device(partner, 1 - core)
    )
    row_out.start()

    for copy in col_out:
        copy.wait_recv()
    highs, sums = [], []
    for d in range(SQUARE):
        for e in range(2):
            slot = 2 * d + e
            value = col_stats[slot]
            order = [SQUARE * w + (k ^ d) for w in range(2) for k in range(SQUARE)]
            if d:
                highs.append(jnp.concatenate([value[k : k + 1] for k in order], axis=0))
                sums.append(jnp.concatenate([value[8 + k : 9 + k] for k in order], axis=0))
            else:
                highs.append(value[:8])
                sums.append(value[8:])
    column_high = functools.reduce(jnp.maximum, highs)
    column_total = sum(s * jnp.exp(h - column_high) for h, s in zip(highs, sums))
    column_factor = 0.5 * jnp.exp(highs[0] - column_high) / column_total

    row_out.wait_recv()
    other = jnp.transpose(jnp.concatenate([row_recv[...]] * (rows // 8), axis=0))
    row_factor = []
    for which in range(2):
        high, total = local[which]
        other_high = other[:, 2 * which : 2 * which + 1]
        other_total = other[:, 2 * which + 1 : 2 * which + 2]
        top = jnp.maximum(high, other_high)
        everything = total * jnp.exp(high - top) + other_total * jnp.exp(other_high - top)
        common = 0.5 * jnp.exp(high - top) / everything
        row_factor.append([common * s for s in scale[which]])

    share = None
    for d in range(SQUARE):
        weights = (
            er_s[d] * row_factor[0][d] - er_t[d] * row_factor[1][d]
        ) + (
            ec_s[d] * column_factor[d : d + 1] - ec_t[d] * column_factor[SQUARE + d : SQUARE + d + 1]
        )
        product = jnp.dot(
            weights.astype(jnp.bfloat16), txt_s[d], preferred_element_type=jnp.float32
        )
        share = product if share is None else share + product

    a_out = remote(part_a, part_a, a_send.at[0], a_recv.at[0], sibling)
    b_out = []
    for h in range(2):
        at = pl.ds(h * half, half)
        b_out.append(
            remote(part_c.at[at], part_b.at[at], b_send.at[h], b_recv.at[0], device(partner, h))
        )

    @pl.when(core == 0)
    def _():
        part_a[...] = share
        a_out.start()

    @pl.when(core == 1)
    def _():
        part_c[...] = share.astype(part_c.dtype)
        for copy in b_out:
            copy.start()

    remote(part_b.at[mine], part_b.at[mine], b_send.at[0], b_recv.at[0], sibling).wait_recv()
    b_forward = remote(part_b.at[mine], part_b.at[mine], b_send.at[2], b_recv.at[1], sibling)
    b_forward.start()

    @pl.when(core == 1)
    def _():
        a_out.wait_recv()

    remote(part_b.at[theirs], part_b.at[theirs], b_send.at[2], b_recv.at[1], sibling).wait_recv()
    out_ref[...] = part_a[...] + part_b[...].astype(jnp.float32)

    for copy in img_out + text_out[1] + text_out[2] + text_out[3] + col_out:
        copy.wait_send()
    for copy in forward.values():
        copy.wait_send()
    row_out.wait_send()
    b_forward.wait_send()

    @pl.when(core == 0)
    def _():
        a_out.wait_send()

    @pl.when(core == 1)
    def _():
        for copy in b_out:
            copy.wait_send()


def eight_chips(img_student, txt_student, img_teacher, txt_teacher):
    rows, narrow = img_student.shape
    wide = img_teacher.shape[1]
    dma = pltpu.SemaphoreType.DMA
    tiles = pltpu.VMEM((SQUARE, rows, rows), jnp.float32)
    partial = pltpu.VMEM((rows, narrow), jnp.float32)
    travelling = pltpu.VMEM((rows, narrow), jnp.bfloat16)
    return pl.pallas_call(
        exchange_kernel,
        out_shape=pltpu.VMEM((rows, narrow), jnp.float32),
        in_specs=[pl.BlockSpec(memory_space=pltpu.HBM)] * 4,
        out_specs=pl.BlockSpec(memory_space=pltpu.VMEM),
        scratch_shapes=[
            pltpu.VMEM((SQUARE, rows, narrow), jnp.bfloat16),
            pltpu.VMEM((SQUARE, rows, wide), jnp.bfloat16),
            pltpu.VMEM((rows, narrow), jnp.bfloat16),
            pltpu.VMEM((rows, wide), jnp.bfloat16),
            tiles, tiles, tiles, tiles,
            pltpu.VMEM((2 * SQUARE, 16, rows), jnp.float32),
            pltpu.VMEM((8, rows), jnp.float32),
            pltpu.VMEM((8, rows), jnp.float32),
            partial, travelling, travelling,
            dma((4,)),
            dma((2, SQUARE)), dma((2, SQUARE)), dma((2, SQUARE)), dma((2, SQUARE)),
            dma((2,)), dma((2, 2)),
            dma((2 * SQUARE,)), dma((2 * SQUARE,)), dma((1,)), dma((1,)),
            dma((1,)), dma((1,)), dma((3,)), dma((2,)),
        ],
        compiler_params=pltpu.CompilerParams(
            collective_id=0, has_side_effects=True, vmem_limit_bytes=60 * 1024 * 1024
        ),
        cost_estimate=pl.CostEstimate(
            flops=2 * rows * SQUARE * rows * (2 * narrow + wide),
            bytes_accessed=8 * rows * (narrow + wide),
            transcendentals=4 * SQUARE * rows * rows,
        ),
    )(img_student, txt_student, img_teacher, txt_teacher)


def solution(mesh):
    placed = P(("parts", "group"), None)

    def per_device(img_student, txt_student, img_teacher, txt_teacher):
        fits = (
            mesh.shape["group"] == 8
            and mesh.shape["blk"] == 2
            and img_student.shape[0] == 128
            and txt_student.shape[0] == 128
        )
        run = eight_chips if fits else general
        return run(img_student, txt_student, img_teacher, txt_teacher)

    return jax.shard_map(
        per_device,
        mesh=mesh,
        in_specs=(placed,) * 4,
        out_specs=placed,
        check_vma=False,
    )
```

```python
import functools

import jax
import jax.numpy as jnp
from jax import lax
from jax.experimental import pallas as pl
from jax.experimental.pallas import tpu as pltpu
from jax.sharding import PartitionSpec as P


def merged_2(value, axis, join):
    pieces = jax.tree.map(lambda part: lax.all_gather(part, axis), value)
    head = jax.tree.map(lambda part: part[0], pieces)
    tail = jax.tree.map(lambda part: part[1:], pieces)
    so_far, _ = lax.scan(lambda so_far, piece: (join(so_far, piece), None), head, tail)
    return so_far


def combine(earlier, later):
    merged = []
    for which in (0, 2):
        highest = jnp.maximum(earlier[which], later[which])
        total = earlier[which + 1] * jnp.exp(earlier[which] - highest) + later[which + 1] * jnp.exp(
            later[which] - highest
        )
        merged.append(highest)
        merged.append(total)
    return tuple(merged)


def general(img_student, txt_student, img_teacher, txt_teacher):
    half_rows = img_student.shape[0] // 2
    side = lax.axis_index("blk")
    begin = side * half_rows
    text_student_own = lax.dynamic_slice_in_dim(txt_student, begin, half_rows, 0)
    text_teacher_own = lax.dynamic_slice_in_dim(txt_teacher, begin, half_rows, 0)
    contract = (((1,), (1,)), ((), ()))
    text_student, text_teacher = (
        lax.all_gather(text_student_own, "group", axis=0, tiled=True),
        lax.all_gather(text_teacher_own, "group", axis=0, tiled=True),
    )
    student = lax.dot_general(
        img_student, text_student, contract, preferred_element_type=jnp.float32
    )
    teacher = lax.dot_general(
        img_teacher, text_teacher, contract, preferred_element_type=jnp.float32
    )
    row_student_high = jnp.max(student, axis=1)
    row_teacher_high = jnp.max(teacher, axis=1)
    row_stats = (
        row_student_high,
        jnp.sum(jnp.exp(student - row_student_high[:, None]), axis=1),
        row_teacher_high,
        jnp.sum(jnp.exp(teacher - row_teacher_high[:, None]), axis=1),
    )
    row_all = merged_2(row_stats, "blk", combine)
    row_student = (row_all[0] + jnp.log(row_all[1]))[:, None]
    row_teacher = (row_all[2] + jnp.log(row_all[3]))[:, None]
    column_student_high = jnp.max(student, axis=0)
    column_teacher_high = jnp.max(teacher, axis=0)
    column_stats = (
        column_student_high,
        jnp.sum(jnp.exp(student - column_student_high[None, :]), axis=0),
        column_teacher_high,
        jnp.sum(jnp.exp(teacher - column_teacher_high[None, :]), axis=0),
    )
    totals = merged_2(column_stats, "group", combine)
    column_student = (totals[0] + jnp.log(totals[1]))[None, :]
    column_teacher = (totals[2] + jnp.log(totals[3]))[None, :]
    row_part = jnp.exp(student - row_student) - jnp.exp(teacher - row_teacher)
    column_part = jnp.exp(student - column_student) - jnp.exp(teacher - column_teacher)
    weights = (0.5 * (row_part + column_part)).astype(jnp.bfloat16)
    partial_image = jnp.dot(weights, text_student, preferred_element_type=jnp.float32)
    return lax.psum(partial_image, "blk")


MESH = pl.DeviceIdType.MESH
SQUARE = 4


def exchange_kernel(
    img_s_hbm, txt_s_hbm, img_t_hbm, txt_t_hbm, out_ref,
    txt_s, txt_t, img_s, img_t,
    er_s, er_t, ec_s, ec_t,
    col_stats, row_send, row_recv, part_a, part_b, part_c,
    local_sem,
    txt_send, txt_recv, fwd_send, fwd_recv,
    img_send, img_recv,
    col_send, col_recv, row_send_sem, row_recv_sem,
    a_send, a_recv, b_send, b_recv,
):
    rows = img_s.shape[0]
    half = rows // 2
    group = lax.axis_index("group")
    core = lax.axis_index("blk")
    x = lax.rem(group, 2)
    b = lax.rem(group // 2, 2)
    a = group // 4

    def chip(d, other_half=0):
        return (
            lax.rem(a + other_half, 2) * 4
            + lax.rem(b + d // 2, 2) * 2
            + lax.rem(x + d % 2, 2)
        )

    def device(chip_index, core_index):
        return {"blk": core_index, "group": chip_index}

    sibling = device(group, 1 - core)
    partner = chip(0, 1)

    def remote(src, dst, send, recv, target):
        return pltpu.make_async_remote_copy(
            src_ref=src, dst_ref=dst, send_sem=send, recv_sem=recv,
            device_id=target, device_id_type=MESH,
        )

    mine = pl.ds(pl.multiple_of(core * half, half), half)
    theirs = pl.ds(pl.multiple_of((1 - core) * half, half), half)

    own = [
        pltpu.make_async_copy(txt_s_hbm, txt_s.at[0], local_sem.at[0]),
        pltpu.make_async_copy(txt_t_hbm, txt_t.at[0], local_sem.at[1]),
    ]
    own_img = [
        pltpu.make_async_copy(img_s_hbm, img_s, local_sem.at[2]),
        pltpu.make_async_copy(img_t_hbm, img_t, local_sem.at[3]),
    ]
    for copy in own:
        copy.start()

    @pl.when(core == 0)
    def _():
        for copy in own_img:
            copy.start()

    barrier = pltpu.get_barrier_semaphore()
    greeted = [sibling, device(partner, core), device(partner, 1 - core)]
    for d in range(1, SQUARE):
        greeted += [device(chip(d), core), device(chip(d), 1 - core)]
    for target in greeted:
        pl.semaphore_signal(barrier, inc=1, device_id=target, device_id_type=MESH)
    pl.semaphore_wait(barrier, len(greeted))

    img_out = [
        remote(img_s_hbm.at[mine], img_s.at[mine], img_send.at[0], img_recv.at[0, core], device(partner, 1)),
        remote(img_t_hbm.at[mine], img_t.at[mine], img_send.at[1], img_recv.at[1, core], device(partner, 1)),
    ]
    text_out = {}
    for d in range(1, SQUARE):
        text_out[d] = [
            remote(txt_s_hbm.at[mine], txt_s.at[d, mine], txt_send.at[0, d], txt_recv.at[0, d], device(chip(d), core)),
        ]
    for d in (1, 2):
        text_out[d].append(
            remote(txt_t_hbm.at[mine], txt_t.at[d, mine], txt_send.at[1, d], txt_recv.at[1, d], device(chip(d), core))
        )
    text_out[3].append(remote(
        txt_t.at[2, mine], txt_t.at[3, mine], txt_send.at[1, 3], txt_recv.at[1, 3], device(chip(1), core)
    ))
    ahead = [text_out[1][1], text_out[1][0], text_out[2][1], text_out[3][0]]
    for copy in img_out + ahead:
        copy.start()
    for copy in img_out:
        copy.wait_send()
    text_out[2][0].start()

    forward = {}

    def pass_on(d, which):
        ref = (txt_s, txt_t)[which]
        text_out[d][which].wait_recv()
        if (d, which) == (2, 1):
            text_out[3][1].start()
        copy = remote(
            ref.at[d, mine], ref.at[d, mine],
            fwd_send.at[which, d], fwd_recv.at[which, d], sibling,
        )
        copy.start()
        forward[d, which] = copy

    contract = (((1,), (1,)), ((), ()))
    row_stats = []

    def tile(d):
        if d == 0:
            for copy in own:
                copy.wait()
        else:
            for which, ref in ((0, txt_s), (1, txt_t)):
                remote(
                    ref.at[d, theirs], ref.at[d, theirs],
                    fwd_send.at[which, d], fwd_recv.at[which, d], sibling,
                ).wait_recv()
        found = []
        for which, (img, txt, er, ec) in enumerate(
            ((img_s, txt_s, er_s, ec_s), (img_t, txt_t, er_t, ec_t))
        ):
            logits = lax.dot_general(
                img[...], txt[d], contract, preferred_element_type=jnp.float32
            )
            row_high = jnp.max(logits, axis=1, keepdims=True)
            row_exp = jnp.exp(logits - row_high)
            er[d] = row_exp
            found.append((row_high, jnp.sum(row_exp, axis=1, keepdims=True)))
            column_high = jnp.max(logits, axis=0, keepdims=True)
            column_exp = jnp.exp(logits - column_high)
            ec[d] = column_exp
            at = which * SQUARE + d
            col_stats[0, at : at + 1, :] = column_high
            col_stats[0, 8 + at : 9 + at, :] = jnp.sum(column_exp, axis=0, keepdims=True)
        row_stats.append(found)

    pass_on(2, 1)
    pass_on(1, 1)
    pass_on(1, 0)
    pass_on(2, 0)

    @pl.when(core == 0)
    def _():
        for copy in own_img:
            copy.wait()

    @pl.when(core == 1)
    def _():
        for h in range(2):
            at = pl.ds(h * half, half)
            for which, ref in ((0, img_s), (1, img_t)):
                remote(
                    ref.at[at], ref.at[at], img_send.at[which], img_recv.at[which, h], device(partner, 1)
                ).wait_recv()

    tile(0)
    pass_on(3, 0)
    pass_on(3, 1)
    tile(1)
    tile(2)
    tile(3)

    col_out = []
    for d in range(SQUARE):
        for e in range(2):
            slot = 2 * d + e
            if slot:
                target = device(chip(d), core if e == 0 else 1 - core)
                copy = remote(
                    col_stats.at[0], col_stats.at[slot], col_send.at[slot], col_recv.at[slot], target
                )
                copy.start()
                col_out.append(copy)

    lane = lax.broadcasted_iota(jnp.int32, (rows, rows), 1)
    packed = jnp.zeros((rows, rows), jnp.float32)
    scale = []
    local = []
    for which in range(2):
        highs = [found[which][0] for found in row_stats]
        high = functools.reduce(jnp.maximum, highs)
        scales = [jnp.exp(h - high) for h in highs]
        total = sum(s * found[which][1] for s, found in zip(scales, row_stats))
        packed = jnp.where(lane == 2 * which, high, packed)
        packed = jnp.where(lane == 2 * which + 1, total, packed)
        scale.append(scales)
        local.append((high, total))
    row_send[...] = jnp.transpose(packed)[:8, :]
    row_out = remote(
        row_send, row_recv, row_send_sem.at[0], row_recv_sem.at[0], device(partner, 1 - core)
    )
    row_out.start()

    for copy in col_out:
        copy.wait_recv()
    highs, sums = [], []
    for d in range(SQUARE):
        for e in range(2):
            slot = 2 * d + e
            value = col_stats[slot]
            order = [SQUARE * w + (k ^ d) for w in range(2) for k in range(SQUARE)]
            if d:
                highs.append(jnp.concatenate([value[k : k + 1] for k in order], axis=0))
                sums.append(jnp.concatenate([value[8 + k : 9 + k] for k in order], axis=0))
            else:
                highs.append(value[:8])
                sums.append(value[8:])
    column_high = functools.reduce(jnp.maximum, highs)
    column_total = sum(s * jnp.exp(h - column_high) for h, s in zip(highs, sums))
    column_factor = 0.5 * jnp.exp(highs[0] - column_high) / column_total

    row_out.wait_recv()
    other = jnp.transpose(jnp.concatenate([row_recv[...]] * (rows // 8), axis=0))
    row_factor = []
    for which in range(2):
        high, total = local[which]
        other_high = other[:, 2 * which : 2 * which + 1]
        other_total = other[:, 2 * which + 1 : 2 * which + 2]
        top = jnp.maximum(high, other_high)
        everything = total * jnp.exp(high - top) + other_total * jnp.exp(other_high - top)
        common = 0.5 * jnp.exp(high - top) / everything
        row_factor.append([common * s for s in scale[which]])

    share = None
    for d in range(SQUARE):
        weights = (
            er_s[d] * row_factor[0][d] - er_t[d] * row_factor[1][d]
        ) + (
            ec_s[d] * column_factor[d : d + 1] - ec_t[d] * column_factor[SQUARE + d : SQUARE + d + 1]
        )
        product = jnp.dot(
            weights.astype(jnp.bfloat16), txt_s[d], preferred_element_type=jnp.float32
        )
        share = product if share is None else share + product

    a_out = remote(part_a, part_a, a_send.at[0], a_recv.at[0], sibling)
    b_out = []
    for h in range(2):
        at = pl.ds(h * half, half)
        b_out.append(
            remote(part_c.at[at], part_b.at[at], b_send.at[h], b_recv.at[0], device(partner, h))
        )

    @pl.when(core == 0)
    def _():
        part_a[...] = share
        a_out.start()

    @pl.when(core == 1)
    def _():
        part_c[...] = share.astype(part_c.dtype)
        for copy in b_out:
            copy.start()

    remote(part_b.at[mine], part_b.at[mine], b_send.at[0], b_recv.at[0], sibling).wait_recv()
    b_forward = remote(part_b.at[mine], part_b.at[mine], b_send.at[2], b_recv.at[1], sibling)
    b_forward.start()

    @pl.when(core == 1)
    def _():
        a_out.wait_recv()

    remote(part_b.at[theirs], part_b.at[theirs], b_send.at[2], b_recv.at[1], sibling).wait_recv()
    out_ref[...] = part_a[...] + part_b[...].astype(jnp.float32)

    for copy in text_out[1] + text_out[2] + text_out[3] + col_out:
        copy.wait_send()
    for copy in forward.values():
        copy.wait_send()
    row_out.wait_send()
    b_forward.wait_send()

    @pl.when(core == 0)
    def _():
        a_out.wait_send()

    @pl.when(core == 1)
    def _():
        for copy in b_out:
            copy.wait_send()


def eight_chips(img_student, txt_student, img_teacher, txt_teacher):
    rows, narrow = img_student.shape
    wide = img_teacher.shape[1]
    dma = pltpu.SemaphoreType.DMA
    tiles = pltpu.VMEM((SQUARE, rows, rows), jnp.float32)
    partial = pltpu.VMEM((rows, narrow), jnp.float32)
    travelling = pltpu.VMEM((rows, narrow), jnp.bfloat16)
    return pl.pallas_call(
        exchange_kernel,
        out_shape=pltpu.VMEM((rows, narrow), jnp.float32),
        in_specs=[pl.BlockSpec(memory_space=pltpu.HBM)] * 4,
        out_specs=pl.BlockSpec(memory_space=pltpu.VMEM),
        scratch_shapes=[
            pltpu.VMEM((SQUARE, rows, narrow), jnp.bfloat16),
            pltpu.VMEM((SQUARE, rows, wide), jnp.bfloat16),
            pltpu.VMEM((rows, narrow), jnp.bfloat16),
            pltpu.VMEM((rows, wide), jnp.bfloat16),
            tiles, tiles, tiles, tiles,
            pltpu.VMEM((2 * SQUARE, 16, rows), jnp.float32),
            pltpu.VMEM((8, rows), jnp.float32),
            pltpu.VMEM((8, rows), jnp.float32),
            partial, travelling, travelling,
            dma((4,)),
            dma((2, SQUARE)), dma((2, SQUARE)), dma((2, SQUARE)), dma((2, SQUARE)),
            dma((2,)), dma((2, 2)),
            dma((2 * SQUARE,)), dma((2 * SQUARE,)), dma((1,)), dma((1,)),
            dma((1,)), dma((1,)), dma((3,)), dma((2,)),
        ],
        compiler_params=pltpu.CompilerParams(
            collective_id=0, has_side_effects=True, vmem_limit_bytes=60 * 1024 * 1024
        ),
        cost_estimate=pl.CostEstimate(
            flops=2 * rows * SQUARE * rows * (2 * narrow + wide),
            bytes_accessed=8 * rows * (narrow + wide),
            transcendentals=4 * SQUARE * rows * rows,
        ),
    )(img_student, txt_student, img_teacher, txt_teacher)


def solution(mesh):
    placed = P(("parts", "group"), None)

    def per_device(img_student, txt_student, img_teacher, txt_teacher):
        fits = (
            mesh.shape["group"] == 8
            and mesh.shape["blk"] == 2
            and img_student.shape[0] == 128
            and txt_student.shape[0] == 128
        )
        run = eight_chips if fits else general
        return run(img_student, txt_student, img_teacher, txt_teacher)

    return jax.shard_map(
        per_device,
        mesh=mesh,
        in_specs=(placed,) * 4,
        out_specs=placed,
        check_vma=False,
    )
```

```python
import functools

import jax
import jax.numpy as jnp
from jax import lax
from jax.experimental import pallas as pl
from jax.experimental.pallas import tpu as pltpu
from jax.sharding import PartitionSpec as P


def merged_2(value, axis, join):
    pieces = jax.tree.map(lambda part: lax.all_gather(part, axis), value)
    head = jax.tree.map(lambda part: part[0], pieces)
    tail = jax.tree.map(lambda part: part[1:], pieces)
    so_far, _ = lax.scan(lambda so_far, piece: (join(so_far, piece), None), head, tail)
    return so_far


def combine(earlier, later):
    merged = []
    for which in (0, 2):
        highest = jnp.maximum(earlier[which], later[which])
        total = earlier[which + 1] * jnp.exp(earlier[which] - highest) + later[which + 1] * jnp.exp(
            later[which] - highest
        )
        merged.append(highest)
        merged.append(total)
    return tuple(merged)


def general(img_student, txt_student, img_teacher, txt_teacher):
    half_rows = img_student.shape[0] // 2
    side = lax.axis_index("blk")
    begin = side * half_rows
    text_student_own = lax.dynamic_slice_in_dim(txt_student, begin, half_rows, 0)
    text_teacher_own = lax.dynamic_slice_in_dim(txt_teacher, begin, half_rows, 0)
    contract = (((1,), (1,)), ((), ()))
    text_student, text_teacher = (
        lax.all_gather(text_student_own, "group", axis=0, tiled=True),
        lax.all_gather(text_teacher_own, "group", axis=0, tiled=True),
    )
    student = lax.dot_general(
        img_student, text_student, contract, preferred_element_type=jnp.float32
    )
    teacher = lax.dot_general(
        img_teacher, text_teacher, contract, preferred_element_type=jnp.float32
    )
    row_student_high = jnp.max(student, axis=1)
    row_teacher_high = jnp.max(teacher, axis=1)
    row_stats = (
        row_student_high,
        jnp.sum(jnp.exp(student - row_student_high[:, None]), axis=1),
        row_teacher_high,
        jnp.sum(jnp.exp(teacher - row_teacher_high[:, None]), axis=1),
    )
    row_all = merged_2(row_stats, "blk", combine)
    row_student = (row_all[0] + jnp.log(row_all[1]))[:, None]
    row_teacher = (row_all[2] + jnp.log(row_all[3]))[:, None]
    column_student_high = jnp.max(student, axis=0)
    column_teacher_high = jnp.max(teacher, axis=0)
    column_stats = (
        column_student_high,
        jnp.sum(jnp.exp(student - column_student_high[None, :]), axis=0),
        column_teacher_high,
        jnp.sum(jnp.exp(teacher - column_teacher_high[None, :]), axis=0),
    )
    totals = merged_2(column_stats, "group", combine)
    column_student = (totals[0] + jnp.log(totals[1]))[None, :]
    column_teacher = (totals[2] + jnp.log(totals[3]))[None, :]
    row_part = jnp.exp(student - row_student) - jnp.exp(teacher - row_teacher)
    column_part = jnp.exp(student - column_student) - jnp.exp(teacher - column_teacher)
    weights = (0.5 * (row_part + column_part)).astype(jnp.bfloat16)
    partial_image = jnp.dot(weights, text_student, preferred_element_type=jnp.float32)
    return lax.psum(partial_image, "blk")


MESH = pl.DeviceIdType.MESH
SQUARE = 4


def exchange_kernel(
    img_s_hbm, txt_s_hbm, img_t_hbm, txt_t_hbm, out_ref,
    txt_s, txt_t, img_s, img_t,
    er_s, er_t, ec_s, ec_t,
    col_stats, row_send, row_recv, part_a, part_b, part_c,
    local_sem,
    txt_send, txt_recv, fwd_send, fwd_recv,
    img_send, img_recv,
    col_send, col_recv, row_send_sem, row_recv_sem,
    a_send, a_recv, b_send, b_recv,
):
    rows = img_s.shape[0]
    half = rows // 2
    group = lax.axis_index("group")
    core = lax.axis_index("blk")
    x = lax.rem(group, 2)
    b = lax.rem(group // 2, 2)
    a = group // 4

    def chip(d, other_half=0):
        return (
            lax.rem(a + other_half, 2) * 4
            + lax.rem(b + d // 2, 2) * 2
            + lax.rem(x + d % 2, 2)
        )

    def device(chip_index, core_index):
        return {"blk": core_index, "group": chip_index}

    sibling = device(group, 1 - core)
    partner = chip(0, 1)

    def remote(src, dst, send, recv, target):
        return pltpu.make_async_remote_copy(
            src_ref=src, dst_ref=dst, send_sem=send, recv_sem=recv,
            device_id=target, device_id_type=MESH,
        )

    mine = pl.ds(pl.multiple_of(core * half, half), half)
    theirs = pl.ds(pl.multiple_of((1 - core) * half, half), half)

    own = [
        pltpu.make_async_copy(txt_s_hbm, txt_s.at[0], local_sem.at[0]),
        pltpu.make_async_copy(txt_t_hbm, txt_t.at[0], local_sem.at[1]),
    ]
    own_img = [
        pltpu.make_async_copy(img_s_hbm, img_s, local_sem.at[2]),
        pltpu.make_async_copy(img_t_hbm, img_t, local_sem.at[3]),
    ]
    for copy in own:
        copy.start()

    @pl.when(core == 0)
    def _():
        for copy in own_img:
            copy.start()

    barrier = pltpu.get_barrier_semaphore()
    greeted = [sibling, device(partner, core), device(partner, 1 - core)]
    for d in range(1, SQUARE):
        greeted += [device(chip(d), core), device(chip(d), 1 - core)]
    for target in greeted:
        pl.semaphore_signal(barrier, inc=1, device_id=target, device_id_type=MESH)
    pl.semaphore_wait(barrier, len(greeted))

    img_out = [
        remote(img_s_hbm.at[mine], img_s.at[mine], img_send.at[0], img_recv.at[0, core], device(partner, 1)),
        remote(img_t_hbm.at[mine], img_t.at[mine], img_send.at[1], img_recv.at[1, core], device(partner, 1)),
    ]
    text_out = {}
    for d in range(1, SQUARE):
        text_out[d] = [
            remote(txt_s_hbm.at[mine], txt_s.at[d, mine], txt_send.at[0, d], txt_recv.at[0, d], device(chip(d), core)),
        ]
    for d in (1, 2):
        text_out[d].append(
            remote(txt_t_hbm.at[mine], txt_t.at[d, mine], txt_send.at[1, d], txt_recv.at[1, d], device(chip(d), core))
        )
    text_out[3].append(remote(
        txt_t.at[2, mine], txt_t.at[3, mine], txt_send.at[1, 3], txt_recv.at[1, 3], device(chip(1), core)
    ))
    ahead = [text_out[1][1], text_out[1][0], text_out[2][1], text_out[3][0]]
    for copy in img_out + ahead:
        copy.start()
    for copy in img_out:
        copy.wait_send()
    text_out[2][0].start()

    forward = {}

    def pass_on(d, which):
        ref = (txt_s, txt_t)[which]
        text_out[d][which].wait_recv()
        if (d, which) == (2, 1):
            text_out[3][1].start()
        copy = remote(
            ref.at[d, mine], ref.at[d, mine],
            fwd_send.at[which, d], fwd_recv.at[which, d], sibling,
        )
        copy.start()
        forward[d, which] = copy

    contract = (((1,), (1,)), ((), ()))
    row_stats = []
    own_highs = [[], []]

    def tile(d):
        if d == 0:
            for copy in own:
                copy.wait()
        else:
            for which, ref in ((0, txt_s), (1, txt_t)):
                remote(
                    ref.at[d, theirs], ref.at[d, theirs],
                    fwd_send.at[which, d], fwd_recv.at[which, d], sibling,
                ).wait_recv()
        found = []
        for which, (img, txt, er, ec) in enumerate(
            ((img_s, txt_s, er_s, ec_s), (img_t, txt_t, er_t, ec_t))
        ):
            logits = lax.dot_general(
                img[...], txt[d], contract, preferred_element_type=jnp.float32
            )
            row_high = jnp.max(logits, axis=1, keepdims=True)
            row_exp = jnp.exp(logits - row_high)
            er[d] = row_exp
            found.append((row_high, jnp.sum(row_exp, axis=1, keepdims=True)))
            column_high = jnp.max(logits, axis=0, keepdims=True)
            column_exp = jnp.exp(logits - column_high)
            ec[d] = column_exp
            at = which * SQUARE + d
            own_highs[which].append(column_high)
            col_stats[0, at : at + 1, :] = column_high + jnp.log(
                jnp.sum(column_exp, axis=0, keepdims=True)
            )
        row_stats.append(found)

    pass_on(2, 1)
    pass_on(1, 1)
    pass_on(1, 0)
    pass_on(2, 0)

    @pl.when(core == 0)
    def _():
        for copy in own_img:
            copy.wait()

    @pl.when(core == 1)
    def _():
        for h in range(2):
            at = pl.ds(h * half, half)
            for which, ref in ((0, img_s), (1, img_t)):
                remote(
                    ref.at[at], ref.at[at], img_send.at[which], img_recv.at[which, h], device(partner, 1)
                ).wait_recv()

    tile(0)
    pass_on(3, 0)
    pass_on(3, 1)
    tile(1)
    tile(2)
    tile(3)

    col_out = []
    for d in range(SQUARE):
        for e in range(2):
            slot = 2 * d + e
            if slot:
                target = device(chip(d), core if e == 0 else 1 - core)
                copy = remote(
                    col_stats.at[0], col_stats.at[slot], col_send.at[slot], col_recv.at[slot], target
                )
                copy.start()
                col_out.append(copy)

    lane = lax.broadcasted_iota(jnp.int32, (rows, rows), 1)
    packed = jnp.zeros((rows, rows), jnp.float32)
    scale = []
    local = []
    for which in range(2):
        highs = [found[which][0] for found in row_stats]
        high = functools.reduce(jnp.maximum, highs)
        scales = [jnp.exp(h - high) for h in highs]
        total = sum(s * found[which][1] for s, found in zip(scales, row_stats))
        packed = jnp.where(lane == 2 * which, high, packed)
        packed = jnp.where(lane == 2 * which + 1, total, packed)
        scale.append(scales)
        local.append((high, total))
    row_send[...] = jnp.transpose(packed)[:8, :]
    row_out = remote(
        row_send, row_recv, row_send_sem.at[0], row_recv_sem.at[0], device(partner, 1 - core)
    )
    row_out.start()

    for copy in col_out:
        copy.wait_recv()
    totals = []
    for d in range(SQUARE):
        for e in range(2):
            slot = 2 * d + e
            value = col_stats[slot]
            order = [SQUARE * w + (k ^ d) for w in range(2) for k in range(SQUARE)]
            if d:
                value = jnp.concatenate([value[k : k + 1] for k in order], axis=0)
            totals.append(value)
    column_high = functools.reduce(jnp.maximum, totals)
    column_total = sum(jnp.exp(t - column_high) for t in totals)
    own_high = jnp.concatenate(own_highs[0] + own_highs[1], axis=0)
    column_factor = 0.5 * jnp.exp(own_high - column_high) / column_total

    row_out.wait_recv()
    other = jnp.transpose(jnp.concatenate([row_recv[...]] * (rows // 8), axis=0))
    row_factor = []
    for which in range(2):
        high, total = local[which]
        other_high = other[:, 2 * which : 2 * which + 1]
        other_total = other[:, 2 * which + 1 : 2 * which + 2]
        top = jnp.maximum(high, other_high)
        everything = total * jnp.exp(high - top) + other_total * jnp.exp(other_high - top)
        common = 0.5 * jnp.exp(high - top) / everything
        row_factor.append([common * s for s in scale[which]])

    share = None
    for d in range(SQUARE):
        weights = (
            er_s[d] * row_factor[0][d] - er_t[d] * row_factor[1][d]
        ) + (
            ec_s[d] * column_factor[d : d + 1] - ec_t[d] * column_factor[SQUARE + d : SQUARE + d + 1]
        )
        product = jnp.dot(
            weights.astype(jnp.bfloat16), txt_s[d], preferred_element_type=jnp.float32
        )
        share = product if share is None else share + product

    a_out = remote(part_a, part_a, a_send.at[0], a_recv.at[0], sibling)
    b_out = []
    for h in range(2):
        at = pl.ds(h * half, half)
        b_out.append(
            remote(part_c.at[at], part_b.at[at], b_send.at[h], b_recv.at[0], device(partner, h))
        )

    @pl.when(core == 0)
    def _():
        part_a[...] = share
        a_out.start()

    @pl.when(core == 1)
    def _():
        part_c[...] = share.astype(part_c.dtype)
        for copy in b_out:
            copy.start()

    remote(part_b.at[mine], part_b.at[mine], b_send.at[0], b_recv.at[0], sibling).wait_recv()
    b_forward = remote(part_b.at[mine], part_b.at[mine], b_send.at[2], b_recv.at[1], sibling)
    b_forward.start()

    @pl.when(core == 1)
    def _():
        a_out.wait_recv()

    remote(part_b.at[theirs], part_b.at[theirs], b_send.at[2], b_recv.at[1], sibling).wait_recv()
    out_ref[...] = part_a[...] + part_b[...].astype(jnp.float32)

    for copy in text_out[1] + text_out[2] + text_out[3] + col_out:
        copy.wait_send()
    for copy in forward.values():
        copy.wait_send()
    row_out.wait_send()
    b_forward.wait_send()

    @pl.when(core == 0)
    def _():
        a_out.wait_send()

    @pl.when(core == 1)
    def _():
        for copy in b_out:
            copy.wait_send()


def eight_chips(img_student, txt_student, img_teacher, txt_teacher):
    rows, narrow = img_student.shape
    wide = img_teacher.shape[1]
    dma = pltpu.SemaphoreType.DMA
    tiles = pltpu.VMEM((SQUARE, rows, rows), jnp.float32)
    partial = pltpu.VMEM((rows, narrow), jnp.float32)
    travelling = pltpu.VMEM((rows, narrow), jnp.bfloat16)
    return pl.pallas_call(
        exchange_kernel,
        out_shape=pltpu.VMEM((rows, narrow), jnp.float32),
        in_specs=[pl.BlockSpec(memory_space=pltpu.HBM)] * 4,
        out_specs=pl.BlockSpec(memory_space=pltpu.VMEM),
        scratch_shapes=[
            pltpu.VMEM((SQUARE, rows, narrow), jnp.bfloat16),
            pltpu.VMEM((SQUARE, rows, wide), jnp.bfloat16),
            pltpu.VMEM((rows, narrow), jnp.bfloat16),
            pltpu.VMEM((rows, wide), jnp.bfloat16),
            tiles, tiles, tiles, tiles,
            pltpu.VMEM((2 * SQUARE, 8, rows), jnp.float32),
            pltpu.VMEM((8, rows), jnp.float32),
            pltpu.VMEM((8, rows), jnp.float32),
            partial, travelling, travelling,
            dma((4,)),
            dma((2, SQUARE)), dma((2, SQUARE)), dma((2, SQUARE)), dma((2, SQUARE)),
            dma((2,)), dma((2, 2)),
            dma((2 * SQUARE,)), dma((2 * SQUARE,)), dma((1,)), dma((1,)),
            dma((1,)), dma((1,)), dma((3,)), dma((2,)),
        ],
        compiler_params=pltpu.CompilerParams(
            collective_id=0, has_side_effects=True, vmem_limit_bytes=60 * 1024 * 1024
        ),
        cost_estimate=pl.CostEstimate(
            flops=2 * rows * SQUARE * rows * (2 * narrow + wide),
            bytes_accessed=8 * rows * (narrow + wide),
            transcendentals=4 * SQUARE * rows * rows,
        ),
    )(img_student, txt_student, img_teacher, txt_teacher)


def solution(mesh):
    placed = P(("parts", "group"), None)

    def per_device(img_student, txt_student, img_teacher, txt_teacher):
        fits = (
            mesh.shape["group"] == 8
            and mesh.shape["blk"] == 2
            and img_student.shape[0] == 128
            and txt_student.shape[0] == 128
        )
        run = eight_chips if fits else general
        return run(img_student, txt_student, img_teacher, txt_teacher)

    return jax.shard_map(
        per_device,
        mesh=mesh,
        in_specs=(placed,) * 4,
        out_specs=placed,
        check_vma=False,
    )
```
